128 devices in a mesh: gx: 8 (over x, core), gy: 16 (over z, y).
Axes of the slice: x: 4, y: 4, z: 4, core: 2. Of those that a mesh axis runs over, the one named last changes fastest.
Arguments:
- snapshots: bfloat16 [4063232, 256], P(('gx', 'gy'))
- row_counts: int32 [128], P(('gx', 'gy')), may hold values from 1024 to 31744, as said below
- move_list: int32 [128, 16, 3], P(('gx', 'gy')), may hold values from 0 to 120, as said below
Outputs:
- basis: bfloat16 [2097152, 256], P(('gx', 'gy'))
- r_factor: float32 [256, 256], replicated
The draws below stay inside these ranges and needn't reach their ends.
Inputs may be any that keep to these rules, and one draw needn't show every extreme that they name: row_counts[d] = 128 (128 + blocks d sends - blocks d receives); in every gx group one device sends 8 blocks to every other and receives none, and one receives 8 blocks from every other and sends none. The destinations of move_list[d] run over all 16 indices once; the count is 0 towards d itself; each first block is the sum of the counts of the earlier rows of move_list[d].
All inputs are finite; a program needn't handle non-finite values.
Results may differ from the reference program's by a relative error of at most 0.0051.
Values may be sent and summed in bfloat16 or wider, within the bound.
A program may use at most 192 MiB of HBM per device.

```python
import math
import jax
import jax.numpy as jnp
from jax import lax

K = 256
BLK = 128
MOST = 8
BAL = 128
CAPB = 248
N_GX = 8
N_GY = 16


def block_loads(key):
    matrix = jax.random.randint(jax.random.fold_in(key, 11), (N_GX, N_GY, N_GY), 0, MOST + 1)
    heavy_rank = jax.random.randint(jax.random.fold_in(key, 12), (N_GX,), 0, N_GY)
    offset_step = jax.random.randint(jax.random.fold_in(key, 13), (N_GX,), 1, N_GY)
    light_rank = (heavy_rank + offset_step) % N_GY
    positions = jnp.arange(N_GY)
    is_heavy = positions[None, :] == heavy_rank[:, None]
    is_light = positions[None, :] == light_rank[:, None]
    matrix = jnp.where(is_heavy[:, :, None], MOST, matrix)
    matrix = jnp.where(is_heavy[:, None, :], 0, matrix)
    matrix = jnp.where(is_light[:, None, :], MOST, matrix)
    matrix = jnp.where(is_light[:, :, None], 0, matrix)
    matrix = jnp.where(jnp.eye(N_GY, dtype=bool)[None], 0, matrix)
    sent_blocks = jnp.sum(matrix, 2)
    taken_blocks = jnp.sum(matrix, 1)
    row_counts = ((BAL + sent_blocks - taken_blocks) * BLK).reshape(N_GX * N_GY).astype(jnp.int32)
    shuffle_keys = jax.random.split(jax.random.fold_in(key, 14), N_GX * N_GY)
    shuffles = jax.vmap(lambda single: jax.random.permutation(single, N_GY))(shuffle_keys)
    amounts = jnp.take_along_axis(matrix.reshape(N_GX * N_GY, N_GY), shuffles, axis=1)
    block_starts = jnp.cumsum(amounts, 1) - amounts
    move_list = jnp.stack([shuffles, block_starts, amounts], -1).astype(jnp.int32)
    return (row_counts, move_list)


def draw_row_counts(key, part):
    shared = block_loads(key)
    return shared[0]


def draw_move_list(key, part):
    shared = block_loads(key)
    return shared[1]


def draw_snapshots(key, part):
    key = jax.random.fold_in(key, 3)
    row_total = N_GX * N_GY * CAPB * BLK
    noise = jax.random.normal(jax.random.fold_in(key, 1), (row_total, K), jnp.float32)
    row_scale = jnp.exp(jax.random.uniform(jax.random.fold_in(key, 2), (row_total, 1), jnp.float32, 0.0, math.log(10.0)))
    col_scale = jnp.exp(jax.random.uniform(jax.random.fold_in(key, 5), (1, K), jnp.float32, 0.0, math.log(10.0)))
    pairing = jax.random.permutation(jax.random.fold_in(key, 6), N_GX * N_GY)
    owners = pairing[jnp.arange(K) // (K // (N_GX * N_GY))]
    row_device = jnp.arange(row_total) // (CAPB * BLK)
    boost = jnp.where(row_device[:, None] == owners[None, :], 12.0, 1.0)
    return (noise * row_scale * col_scale * boost * 0.1).astype(jnp.bfloat16)


def setup_inputs(seed: int = 0) -> dict:
    key_of = jax.random.split(jax.random.key(seed), 4)
    return {
        "snapshots": draw_snapshots(jax.random.fold_in(key_of[3], 71), 0),
        "row_counts": draw_row_counts(jax.random.fold_in(key_of[3], 71), 0),
        "move_list": draw_move_list(jax.random.fold_in(key_of[3], 71), 0),
    }


def cholesky_lower(gram):
    size = gram.shape[0]
    index = jnp.arange(size, dtype=jnp.int32)

    def step(column_at, carry):
        rest, lower = carry
        column = lax.dynamic_slice_in_dim(rest, column_at, 1, 1)[:, 0]
        pivot = lax.dynamic_slice_in_dim(column, column_at, 1, 0)[0]
        column = jnp.where(index >= column_at, column / jnp.sqrt(pivot), jnp.zeros((), rest.dtype))
        lower = lax.dynamic_update_slice_in_dim(lower, column[:, None], column_at, 1)
        rest = rest - column[:, None] * column[None, :]
        return (rest, lower)
    _, lower = lax.fori_loop(jnp.int32(0), jnp.int32(size), step, (gram, jnp.zeros_like(gram)))
    return lower

def lower_inverse(lower):
    size = lower.shape[0]
    identity = jnp.eye(size, dtype=lower.dtype)

    def step(row_at, solved):
        row_lower = lax.dynamic_slice_in_dim(lower, row_at, 1, 0)
        unit = lax.dynamic_slice_in_dim(identity, row_at, 1, 0)
        pivot = lax.dynamic_slice_in_dim(row_lower[0], row_at, 1, 0)[0]
        new_row = (unit - jnp.dot(row_lower, solved, precision=lax.Precision.HIGHEST)) / pivot
        return lax.dynamic_update_slice_in_dim(solved, new_row, row_at, 0)
    return lax.fori_loop(jnp.int32(0), jnp.int32(size), step, jnp.zeros_like(lower))

def balanced_rows(snapshots, row_counts, move_list):
    destinations = move_list[:, :, 0]
    block_starts = move_list[:, :, 1]
    amounts = move_list[:, :, 2]
    targets = jnp.arange(N_GY, dtype=jnp.int32)
    matches = destinations[:, :, None] == targets[None, None, :]
    sent_to = lax.optimization_barrier(jnp.sum(jnp.where(matches, amounts[:, :, None], 0), 1)).reshape(N_GX, N_GY, N_GY)
    start_to = lax.optimization_barrier(jnp.sum(jnp.where(matches, block_starts[:, :, None], 0), 1)).reshape(N_GX, N_GY, N_GY)
    sent_blocks = lax.optimization_barrier(jnp.sum(sent_to, 2))
    kept_blocks = row_counts.reshape(N_GX, N_GY) // BLK - sent_blocks
    ends = jnp.cumsum(sent_to, 1)
    begins = ends - sent_to
    ends_t = jnp.transpose(ends, (0, 2, 1))
    begins_t = jnp.transpose(begins, (0, 2, 1))
    starts_t = jnp.transpose(start_to, (0, 2, 1))
    positions = jnp.arange(BAL, dtype=jnp.int32)
    remainder = positions[None, None, :] - kept_blocks[:, :, None]
    sources = lax.optimization_barrier(jnp.sum((ends_t[:, :, None, :] <= remainder[:, :, :, None]).astype(jnp.int32), 3))
    sources = jnp.clip(sources, 0, N_GY - 1).astype(jnp.int32)
    inside = remainder - jnp.take_along_axis(begins_t, sources, axis=2)
    moved_block = jnp.take_along_axis(starts_t, sources, axis=2) + inside
    own_block = sent_blocks[:, :, None] + positions[None, None, :]
    group_base = (jnp.arange(N_GX, dtype=jnp.int32) * N_GY)[:, None, None]
    own_device = jnp.broadcast_to(targets[None, :, None], remainder.shape)
    source_device = jnp.where(remainder < 0, own_device, sources) + group_base
    block = jnp.clip(jnp.where(remainder < 0, own_block, moved_block), 0, CAPB - 1)
    flat = (source_device * CAPB + block).reshape(-1).astype(jnp.int32)
    table = snapshots.reshape(N_GX * N_GY * CAPB, BLK, K)
    return table[flat].reshape(N_GX * N_GY, BAL * BLK, K)

def reference(snapshots, row_counts, move_list):
    balanced = balanced_rows(snapshots, row_counts, move_list)

    def add_term(total, piece):
        term = lax.dot_general(piece, piece, (((0,), (0,)), ((), ())), preferred_element_type=jnp.float32)
        return (total + term, None)
    gram, _ = lax.scan(add_term, jnp.zeros((K, K), jnp.float32), balanced)
    lower = cholesky_lower(gram)
    upper = lower.T
    scale = math.sqrt(N_GX * N_GY * BAL * BLK)
    inverse_scaled = (lower_inverse(lower).T * scale).astype(jnp.bfloat16)

    def project(piece):
        return jnp.dot(piece, inverse_scaled, preferred_element_type=jnp.float32).astype(jnp.bfloat16)
    basis = lax.map(project, balanced).reshape(N_GX * N_GY * BAL * BLK, K)
    r_factor = upper / scale
    return (basis, r_factor)
```

```python
import functools
import math

import jax
import jax.numpy as jnp
from jax import lax
from jax.experimental import pallas as pl
from jax.experimental.pallas import tpu as pltpu
from jax.sharding import PartitionSpec as P

K = 256
BLK = 128
MOST = 8
BAL = 128
CAPB = 248
CHUNK = MOST * BLK
CHUNKS = CAPB // MOST
FRONT = BAL // MOST
NZ = NY = 4
GX = 8
SLICE = K // GX
PANEL = 32
PIECE = 2
MESH = pl.DeviceIdType.MESH
HIGH = lax.Precision.HIGHEST

OFFSETS = [(1, 0), (0, 1), (-1, 0), (0, -1), (2, 0), (0, 2), (1, 1), (-1, -1), (1, -1), (-1, 1),
           (2, 1), (1, 2), (2, -1), (-1, 2), (2, 2)]
PEERS = len(OFFSETS)


def rank_at(rank, dz, dy):
    z, y = lax.div(rank, NY), lax.rem(rank, NY)
    return lax.rem(z + (dz + NZ), NZ) * NY + lax.rem(y + (dy + NY), NY)


def cholesky_panels(work, panel_rows):
    rows = lax.broadcasted_iota(jnp.int32, (PANEL, 1), 0)
    all_rows = lax.broadcasted_iota(jnp.int32, (K, 1), 0)

    def panel_step(panel, carry):
        first = pl.multiple_of(panel * PANEL, PANEL)
        block = work[pl.ds(first, PANEL), :]
        diag = pltpu.roll(block[:, :K], K - first, 1)[:, :128]
        for k in range(PANEL):
            inv = lax.rsqrt(diag[k:k + 1, k:k + 1])
            column = diag[:, k:k + 1] * inv
            diag_row = diag[k:k + 1, :] * inv
            block_row = block[k:k + 1, :] * inv
            factor = jnp.where(rows > k, column, 0.0)
            diag = jnp.where(rows == k, diag_row, diag - factor * diag_row)
            block = jnp.where(rows == k, block_row, block - factor * block_row)
        panel_rows[...] = block
        update = lax.dot_general(panel_rows[:, :K], panel_rows[...], (((0,), (0,)), ((), ())),
                                 precision=HIGH, preferred_element_type=jnp.float32)
        work[...] = work[...] - jnp.where(all_rows >= first + PANEL, update, 0.0)
        work[pl.ds(first, PANEL), :] = block
        return carry

    lax.fori_loop(0, K // PANEL, panel_step, 0)


def exchange_kernel(scale, counts_ref, moves_ref, slab_hbm,
                    front, back, arrived, counts_out, inverse_ref, factor_ref,
                    send, count_send, count_recv, gram, gx_recv, y_recv, z_recv, total, work, panel_rows,
                    load_sem, send_sem, recv_sem, cs_sem, cr_sem,
                    gx_s, gx_r, y_s, y_r, z_s, z_r, ag_s, ag_r):
    gx = lax.axis_index("gx")
    gy = lax.axis_index("gy")

    partners = [rank_at(gy, dz, dy) for dz, dy in OFFSETS]
    columns = [lax.rem(gx + d, GX) for d in range(1, GX)]

    def load(chunk):
        here = front.at[pl.ds(chunk * MOST, MOST)] if chunk < FRONT else back.at[pl.ds((chunk - FRONT) * MOST, MOST)]
        return pltpu.make_async_copy(slab_hbm.at[pl.ds(chunk * MOST, MOST)], here, load_sem.at[chunk])

    for chunk in range(CHUNKS):
        load(chunk).start()

    barrier = pltpu.get_barrier_semaphore()
    for to in partners:
        pl.semaphore_signal(barrier, inc=1, device_id=(gx, to), device_id_type=MESH)
    for to in columns:
        pl.semaphore_signal(barrier, inc=1, device_id=(to, gy), device_id_type=MESH)

    starts, amounts = [], []
    for n, to in enumerate(partners):
        start = jnp.int32(0)
        amount = jnp.int32(0)
        for r in range(NZ * NY):
            hit = moves_ref[3 * r] == to
            start = start + jnp.where(hit, moves_ref[3 * r + 1], 0)
            amount = amount + jnp.where(hit, moves_ref[3 * r + 2], 0)
        starts.append(start)
        amounts.append(amount)
        count_send[n] = jnp.full((8, 128), amount, jnp.int32)

    pl.semaphore_wait(barrier, PEERS + GX - 1)

    def count_copy(n):
        return pltpu.make_async_remote_copy(
            src_ref=count_send.at[n], dst_ref=count_recv.at[n], send_sem=cs_sem.at[n], recv_sem=cr_sem.at[n],
            device_id=(gx, partners[n]), device_id_type=MESH)

    for n in range(PEERS):
        count_copy(n).start()
    for chunk in range(FRONT):
        load(chunk).wait()

    def block_copy(n, first, blocks):
        part = pl.ds(first, blocks)
        return pltpu.make_async_remote_copy(
            src_ref=send.at[n, part], dst_ref=arrived.at[n, part], send_sem=send_sem.at[n], recv_sem=recv_sem.at[n],
            device_id=(gx, partners[n]), device_id_type=MESH)

    for h in range(0, MOST, PIECE):
        for n in range(PEERS):
            for b in range(h, h + PIECE):
                send[n, b] = front[starts[n] + b]
            block_copy(n, h, PIECE).start()

    valid_rows = counts_ref[0]
    gram[...] = jnp.zeros_like(gram)

    def gram_add(buffer, chunk, chunks_before):
        pieces = []
        for b in range(MOST):
            block = chunk * MOST + b
            keep = jnp.where((block + chunks_before * MOST) * BLK < valid_rows, 1.0, 0.0)
            keep = jnp.full((1, K), keep, jnp.float32).astype(jnp.bfloat16)
            pieces.append(buffer[block] * keep)
        rows = jnp.concatenate(pieces, axis=0)
        gram[...] += lax.dot_general(rows, rows, (((0,), (0,)), ((), ())), preferred_element_type=jnp.float32)

    def gram_front(chunk, carry):
        gram_add(front, chunk, 0)
        return carry

    def gram_back(chunk, carry):
        gram_add(back, chunk, FRONT)
        return carry

    lax.fori_loop(0, FRONT, gram_front, 0)
    for chunk in range(FRONT, CHUNKS):
        load(chunk).wait()
    lax.fori_loop(0, CHUNKS - FRONT, gram_back, 0)

    def mine(i):
        return pl.ds(pl.multiple_of(i * SLICE, SLICE), SLICE)

    def gx_copy(d):
        to = columns[d - 1]
        return pltpu.make_async_remote_copy(
            src_ref=gram.at[mine(to), :], dst_ref=gx_recv.at[gx], send_sem=gx_s.at[d - 1], recv_sem=gx_r.at[d - 1],
            device_id=(to, gy), device_id_type=MESH)

    for d in range(1, GX):
        gx_copy(d).start()
    gx_recv[gx] = gram[mine(gx), :]
    for d in range(1, GX):
        gx_copy(d).wait()
    part = gx_recv[0]
    for i in range(1, GX):
        part = part + gx_recv[i]

    z, y = lax.div(gy, NY), lax.rem(gy, NY)

    def y_copy(d):
        return pltpu.make_async_remote_copy(
            src_ref=y_recv.at[y], dst_ref=y_recv.at[y], send_sem=y_s.at[d - 1], recv_sem=y_r.at[d - 1],
            device_id=(gx, rank_at(gy, 0, d)), device_id_type=MESH)

    def z_copy(d):
        return pltpu.make_async_remote_copy(
            src_ref=z_recv.at[z], dst_ref=z_recv.at[z], send_sem=z_s.at[d - 1], recv_sem=z_r.at[d - 1],
            device_id=(gx, rank_at(gy, d, 0)), device_id_type=MESH)

    y_recv[y] = part
    for d in range(1, NY):
        y_copy(d).start()
    for d in range(1, NY):
        y_copy(d).wait()
    z_recv[z] = (y_recv[0] + y_recv[1]) + (y_recv[2] + y_recv[3])
    for d in range(1, NZ):
        z_copy(d).start()
    for d in range(1, NZ):
        z_copy(d).wait()
    total[mine(gx), :] = (z_recv[0] + z_recv[1]) + (z_recv[2] + z_recv[3])

    def ag_copy(d):
        return pltpu.make_async_remote_copy(
            src_ref=total.at[mine(gx), :], dst_ref=total.at[mine(gx), :], send_sem=ag_s.at[d - 1], recv_sem=ag_r.at[d - 1],
            device_id=(columns[d - 1], gy), device_id_type=MESH)

    for d in range(1, GX):
        ag_copy(d).start()
    for d in range(1, GX):
        ag_copy(d).wait()

    row = lax.broadcasted_iota(jnp.int32, (K, K), 0)
    col = lax.broadcasted_iota(jnp.int32, (K, K), 1)
    work[:, :K] = total[...]
    work[:, K:] = jnp.where(row == col, 1.0, 0.0)
    cholesky_panels(work, panel_rows)
    factor_ref[...] = jnp.where(col >= row, work[:, :K], 0.0) * (1.0 / scale)
    inverse_ref[...] = (work[:, K:].T * scale).astype(jnp.bfloat16)

    for n in range(PEERS):
        count_copy(n).wait()
    lane = lax.broadcasted_iota(jnp.int32, (8, 128), 1)
    gathered = jnp.zeros((8, 128), jnp.int32)
    for n in range(PEERS):
        gathered = jnp.where(lane == n, count_recv[n], gathered)
    counts_out[...] = gathered
    for n in range(PEERS):
        block_copy(n, 0, MOST).wait()


def basis_kernel(counts_ref, moves_ref, came_ref, front, back, arrived, inverse_ref, factor_ref,
                 basis_hbm, r_ref, source, rows, out, out_sem):
    gy = lax.axis_index("gy")
    sent = jnp.int32(0)
    for r in range(NZ * NY):
        sent = sent + moves_ref[3 * r + 2]
    kept = counts_ref[0] // BLK - sent

    at = kept
    for j in range(NZ * NY):
        dz = lax.rem(lax.div(gy, NY) + (NZ - j // NY), NZ)
        dy = lax.rem(lax.rem(gy, NY) + (NY - j % NY), NY)
        slot = jnp.int32(0)
        for n, (oz, oy) in enumerate(OFFSETS):
            slot = jnp.where((dz == oz % NZ) & (dy == oy % NY), n, slot)
        amount = jnp.where((dz == 0) & (dy == 0), 0, came_ref[0, slot])

        def note(k, carry):
            source[at + k] = slot * MOST + k
            return carry

        lax.fori_loop(0, amount, note, 0)
        at = at + amount

    r_ref[...] = factor_ref[...]

    def out_copy(chunk):
        part = pl.ds(pl.multiple_of(chunk * CHUNK, CHUNK), CHUNK)
        return pltpu.make_async_copy(out.at[part, :], basis_hbm.at[part, :], out_sem.at[chunk])

    def chunk_step(chunk, carry):
        for b in range(MOST):
            position = chunk * MOST + b
            own = sent + position
            here = slice(b * BLK, (b + 1) * BLK)

            @pl.when((position < kept) & (own < BAL))
            def _():
                rows[here, :] = front[own]

            @pl.when((position < kept) & (own >= BAL))
            def _():
                rows[here, :] = back[own - BAL]

            @pl.when(position >= kept)
            def _():
                rows[here, :] = arrived[source[position]]

        out[pl.ds(pl.multiple_of(chunk * CHUNK, CHUNK), CHUNK), :] = jnp.dot(
            rows[...], inverse_ref[...], preferred_element_type=jnp.float32).astype(jnp.bfloat16)
        out_copy(chunk).start()
        return carry

    lax.fori_loop(0, FRONT, chunk_step, 0)
    for chunk in range(FRONT):
        out_copy(chunk).wait()


def local(snapshots, row_counts, move_list):
    scale = math.sqrt(lax.axis_size("gx") * lax.axis_size("gy") * BAL * BLK)
    moves = move_list.reshape(NZ * NY * 3)
    smem = pl.BlockSpec(memory_space=pltpu.SMEM)
    vmem = pl.BlockSpec(memory_space=pltpu.VMEM)
    anywhere = pl.BlockSpec(memory_space=pl.ANY)
    dma = pltpu.SemaphoreType.DMA
    f32, bf16 = jnp.float32, jnp.bfloat16
    front, back, arrived, came, inverse, factor = pl.pallas_call(
        functools.partial(exchange_kernel, scale),
        name="exchange",
        out_shape=(
            pltpu.VMEM((BAL, BLK, K), bf16),
            pltpu.VMEM((CAPB - BAL, BLK, K), bf16),
            pltpu.VMEM((PEERS, MOST, BLK, K), bf16),
            jax.ShapeDtypeStruct((8, 128), jnp.int32),
            jax.ShapeDtypeStruct((K, K), bf16),
            jax.ShapeDtypeStruct((K, K), f32),
        ),
        in_specs=[smem, smem, anywhere],
        out_specs=(vmem,) * 6,
        scratch_shapes=[
            pltpu.VMEM((PEERS, MOST, BLK, K), bf16),
            pltpu.VMEM((PEERS, 8, 128), jnp.int32),
            pltpu.VMEM((PEERS, 8, 128), jnp.int32),
            pltpu.VMEM((K, K), f32),
            pltpu.VMEM((GX, SLICE, K), f32),
            pltpu.VMEM((NY, SLICE, K), f32),
            pltpu.VMEM((NZ, SLICE, K), f32),
            pltpu.VMEM((K, K), f32),
            pltpu.VMEM((K, 2 * K), f32),
            pltpu.VMEM((PANEL, 2 * K), f32),
            dma((CHUNKS,)), dma((PEERS,)), dma((PEERS,)), dma((PEERS,)), dma((PEERS,)),
            dma((GX - 1,)), dma((GX - 1,)), dma((NY - 1,)), dma((NY - 1,)), dma((NZ - 1,)), dma((NZ - 1,)),
            dma((GX - 1,)), dma((GX - 1,)),
        ],
        compiler_params=pltpu.CompilerParams(collective_id=0, has_side_effects=True, vmem_limit_bytes=20 << 20),
    )(row_counts, moves, snapshots.reshape(CAPB, BLK, K))
    basis, r_factor = pl.pallas_call(
        basis_kernel,
        name="project",
        out_shape=(jax.ShapeDtypeStruct((BAL * BLK, K), bf16), jax.ShapeDtypeStruct((K, K), f32)),
        in_specs=[smem, smem, smem, vmem, vmem, vmem, vmem, vmem],
        out_specs=(anywhere, vmem),
        scratch_shapes=[
            pltpu.SMEM((BAL,), jnp.int32),
            pltpu.VMEM((CHUNK, K), bf16),
            pltpu.VMEM((BAL * BLK, K), bf16),
            dma((FRONT,)),
        ],
        compiler_params=pltpu.CompilerParams(vmem_limit_bytes=16 << 20),
    )(row_counts, moves, came, front, back, arrived.reshape(PEERS * MOST, BLK, K), inverse, factor)
    return (basis, r_factor)


def solution(mesh):
    in_specs = (P(("gx", "gy"), None), P(("gx", "gy")), P(("gx", "gy"), None, None))
    out_specs = (P(("gx", "gy"), None), P())
    return jax.shard_map(local, mesh=mesh, in_specs=in_specs, out_specs=out_specs, check_vma=False)
```

```python
import functools
import math

import jax
import jax.numpy as jnp
from jax import lax
from jax.experimental import pallas as pl
from jax.experimental.pallas import tpu as pltpu
from jax.sharding import PartitionSpec as P

K = 256
BLK = 128
MOST = 8
BAL = 128
CAPB = 248
CHUNK = MOST * BLK
CHUNKS = CAPB // MOST
FRONT = BAL // MOST
NZ = NY = 4
GX = 8
SLICE = K // GX
PANEL = 32
GROUPS = (1, 1, 1, 1, 4)
MESH = pl.DeviceIdType.MESH
HIGH = lax.Precision.HIGHEST

OFFSETS = [(1, 0), (0, 1), (-1, 0), (0, -1), (2, 0), (0, 2), (1, 1), (-1, -1), (1, -1), (-1, 1),
           (2, 1), (1, 2), (2, -1), (-1, 2), (2, 2)]
PEERS = len(OFFSETS)


def rank_at(rank, dz, dy):
    z, y = lax.div(rank, NY), lax.rem(rank, NY)
    return lax.rem(z + (dz + NZ), NZ) * NY + lax.rem(y + (dy + NY), NY)


def cholesky_panels(work, panel_rows):
    rows = lax.broadcasted_iota(jnp.int32, (PANEL, 1), 0)
    all_rows = lax.broadcasted_iota(jnp.int32, (K, 1), 0)

    def panel_step(panel, carry):
        first = pl.multiple_of(panel * PANEL, PANEL)
        block = work[pl.ds(first, PANEL), :]
        diag = pltpu.roll(block[:, :K], K - first, 1)[:, :128]
        for k in range(PANEL):
            inv = lax.rsqrt(diag[k:k + 1, k:k + 1])
            column = diag[:, k:k + 1] * inv
            diag_row = diag[k:k + 1, :] * inv
            block_row = block[k:k + 1, :] * inv
            factor = jnp.where(rows > k, column, 0.0)
            diag = jnp.where(rows == k, diag_row, diag - factor * diag_row)
            block = jnp.where(rows == k, block_row, block - factor * block_row)
        panel_rows[...] = block
        update = lax.dot_general(panel_rows[:, :K], panel_rows[...], (((0,), (0,)), ((), ())),
                                 precision=HIGH, preferred_element_type=jnp.float32)
        work[...] = work[...] - jnp.where(all_rows >= first + PANEL, update, 0.0)
        work[pl.ds(first, PANEL), :] = block
        return carry

    lax.fori_loop(0, K // PANEL, panel_step, 0)


def exchange_kernel(scale, counts_ref, moves_ref, slab_hbm,
                    pool, where_ref, inverse_ref, factor_ref,
                    front, back, send, count_send, count_recv, gram, gx_recv, y_recv, z_recv, total, work, panel_rows,
                    load_sem, send_sem, recv_sem, cs_sem, cr_sem,
                    gx_s, gx_r, y_s, y_r, z_s, z_r, ag_s, ag_r):
    gx = lax.axis_index("gx")
    gy = lax.axis_index("gy")
    partners = [rank_at(gy, dz, dy) for dz, dy in OFFSETS]
    columns = [lax.rem(gx + d, GX) for d in range(1, GX)]

    def load(chunk, buffer, chunks_before):
        return pltpu.make_async_copy(slab_hbm.at[pl.ds((chunk + chunks_before) * MOST, MOST)],
                                     buffer.at[pl.ds(chunk * MOST, MOST)], load_sem.at[chunk + chunks_before])

    for chunk in range(FRONT):
        load(chunk, front, 0).start()
    for chunk in range(CHUNKS - FRONT):
        load(chunk, back, FRONT).start()

    barrier = pltpu.get_barrier_semaphore()
    for to in partners:
        pl.semaphore_signal(barrier, inc=1, device_id=(gx, to), device_id_type=MESH)
    for to in columns:
        pl.semaphore_signal(barrier, inc=1, device_id=(to, gy), device_id_type=MESH)

    starts, sent = [], jnp.int32(0)
    for n, to in enumerate(partners):
        start = jnp.int32(0)
        amount = jnp.int32(0)
        for r in range(NZ * NY):
            hit = moves_ref[0, 0, r] == to
            start = start + jnp.where(hit, moves_ref[1, 0, r], 0)
            amount = amount + jnp.where(hit, moves_ref[2, 0, r], 0)
        starts.append(start)
        sent = sent + amount
        count_send[n] = jnp.full((8, 128), amount, jnp.int32)

    pl.semaphore_wait(barrier, PEERS + GX - 1)

    def count_copy(n):
        return pltpu.make_async_remote_copy(
            src_ref=count_send.at[n], dst_ref=count_recv.at[n], send_sem=cs_sem.at[n], recv_sem=cr_sem.at[n],
            device_id=(gx, partners[n]), device_id_type=MESH)

    def block_copy(n, first, blocks):
        return pltpu.make_async_remote_copy(
            src_ref=send.at[n, pl.ds(first, blocks)], dst_ref=pool.at[pl.ds(BAL + n * MOST + first, blocks)],
            send_sem=send_sem.at[n], recv_sem=recv_sem.at[n],
            device_id=(gx, partners[n]), device_id_type=MESH)

    def send_blocks(first, blocks):
        for b in range(first, first + blocks):
            for n in range(PEERS):
                send[n, b] = front[starts[n] + b]
                block_copy(n, b, 1).start()

    for chunk in range(FRONT):
        load(chunk, front, 0).wait()
    send_blocks(0, GROUPS[0])
    for n in range(PEERS):
        count_copy(n).start()

    valid_rows = counts_ref[0]
    gram[...] = jnp.zeros_like(gram)

    def gram_add(buffer, chunk, chunks_before):
        pieces = []
        for b in range(MOST):
            block = chunk * MOST + b
            keep = jnp.where((block + chunks_before * MOST) * BLK < valid_rows, 1.0, 0.0)
            keep = jnp.full((1, K), keep, jnp.float32).astype(jnp.bfloat16)
            pieces.append(buffer[block] * keep)
        rows = jnp.concatenate(pieces, axis=0)
        gram[...] += lax.dot_general(rows, rows, (((0,), (0,)), ((), ())), preferred_element_type=jnp.float32)

    def gram_front(chunk, carry):
        gram_add(front, chunk, 0)
        return carry

    def gram_back(chunk, carry):
        load(chunk, back, FRONT).wait()
        gram_add(back, chunk, FRONT)
        return carry

    lax.fori_loop(0, FRONT, gram_front, 0)
    lax.fori_loop(0, CHUNKS - FRONT, gram_back, 0)

    def mine(i):
        return pl.ds(pl.multiple_of(i * SLICE, SLICE), SLICE)

    def gx_copy(d):
        to = columns[d - 1]
        return pltpu.make_async_remote_copy(
            src_ref=gram.at[mine(to), :], dst_ref=gx_recv.at[gx], send_sem=gx_s.at[d - 1], recv_sem=gx_r.at[d - 1],
            device_id=(to, gy), device_id_type=MESH)

    for d in range(1, GX):
        gx_copy(d).start()
    send_blocks(GROUPS[0], GROUPS[1])
    gx_recv[gx] = gram[mine(gx), :]
    for d in range(1, GX):
        gx_copy(d).wait()
    part = gx_recv[0]
    for i in range(1, GX):
        part = part + gx_recv[i]

    z, y = lax.div(gy, NY), lax.rem(gy, NY)

    def y_copy(d):
        return pltpu.make_async_remote_copy(
            src_ref=y_recv.at[y], dst_ref=y_recv.at[y], send_sem=y_s.at[d - 1], recv_sem=y_r.at[d - 1],
            device_id=(gx, rank_at(gy, 0, d)), device_id_type=MESH)

    def z_copy(d):
        return pltpu.make_async_remote_copy(
            src_ref=z_recv.at[z], dst_ref=z_recv.at[z], send_sem=z_s.at[d - 1], recv_sem=z_r.at[d - 1],
            device_id=(gx, rank_at(gy, d, 0)), device_id_type=MESH)

    y_recv[y] = part
    for d in range(1, NY):
        y_copy(d).start()
    send_blocks(sum(GROUPS[:2]), GROUPS[2])
    for d in range(1, NY):
        y_copy(d).wait()
    z_recv[z] = (y_recv[0] + y_recv[1]) + (y_recv[2] + y_recv[3])
    for d in range(1, NZ):
        z_copy(d).start()
    send_blocks(sum(GROUPS[:3]), GROUPS[3])
    for d in range(1, NZ):
        z_copy(d).wait()
    total[mine(gx), :] = (z_recv[0] + z_recv[1]) + (z_recv[2] + z_recv[3])

    def ag_copy(d):
        return pltpu.make_async_remote_copy(
            src_ref=total.at[mine(gx), :], dst_ref=total.at[mine(gx), :], send_sem=ag_s.at[d - 1], recv_sem=ag_r.at[d - 1],
            device_id=(columns[d - 1], gy), device_id_type=MESH)

    for d in range(1, GX):
        ag_copy(d).start()
    send_blocks(sum(GROUPS[:4]), GROUPS[4])
    for d in range(1, GX):
        ag_copy(d).wait()

    row = lax.broadcasted_iota(jnp.int32, (K, K), 0)
    col = lax.broadcasted_iota(jnp.int32, (K, K), 1)
    work[:, :K] = total[...]
    work[:, K:] = jnp.where(row == col, 1.0, 0.0)
    cholesky_panels(work, panel_rows)
    factor_ref[...] = jnp.where(col >= row, work[:, :K], 0.0) * (1.0 / scale)
    inverse_ref[...] = (work[:, K:].T * scale).astype(jnp.bfloat16)

    def keep_block(at, carry):
        block = sent + at
        own = jnp.full((1, K), block, jnp.int32) < BAL
        early = front[jnp.minimum(block, BAL - 1)].astype(jnp.float32)
        late = back[jnp.maximum(block - BAL, 0)].astype(jnp.float32)
        pool[at] = jnp.where(own, early, late).astype(jnp.bfloat16)
        return carry

    lax.fori_loop(0, BAL, keep_block, 0)

    for n in range(PEERS):
        count_copy(n).wait()
    position = lax.broadcasted_iota(jnp.int32, (8, 128), 1)
    rest = position - (lax.div(valid_rows, BLK) - sent)
    where = position
    begin = jnp.zeros((8, 128), jnp.int32)
    for j in range(NZ * NY):
        dz = lax.rem(z + (NZ - j // NY), NZ)
        dy = lax.rem(y + (NY - j % NY), NY)
        slot = jnp.int32(0)
        for n, (oz, oy) in enumerate(OFFSETS):
            slot = jnp.where((dz == oz % NZ) & (dy == oy % NY), n, slot)
        amount = jnp.where(gy == j, 0, count_recv[slot])
        inside = rest - begin
        where = jnp.where((inside >= 0) & (inside < amount), BAL + slot * MOST + inside, where)
        begin = begin + amount
    where_ref[...] = where
    for n in range(PEERS):
        block_copy(n, 0, MOST).wait()


def basis_kernel(where_ref, pool, inverse_ref, factor_ref, basis_hbm, r_ref, out, out_sem):
    def out_copy(chunk):
        part = pl.ds(pl.multiple_of(chunk * CHUNK, CHUNK), CHUNK)
        return pltpu.make_async_copy(out.at[part, :], basis_hbm.at[part, :], out_sem.at[chunk])

    def chunk_step(chunk, carry):
        rows = jnp.concatenate([pool[where_ref[0, chunk * MOST + b]] for b in range(MOST)], axis=0)
        out[pl.ds(pl.multiple_of(chunk * CHUNK, CHUNK), CHUNK), :] = jnp.dot(
            rows, inverse_ref[...], preferred_element_type=jnp.float32).astype(jnp.bfloat16)
        out_copy(chunk).start()
        return carry

    lax.fori_loop(0, FRONT, chunk_step, 0)
    r_ref[...] = factor_ref[...]
    for chunk in range(FRONT):
        out_copy(chunk).wait()


def local(snapshots, row_counts, move_list):
    scale = math.sqrt(lax.axis_size("gx") * lax.axis_size("gy") * BAL * BLK)
    smem = pl.BlockSpec(memory_space=pltpu.SMEM)
    vmem = pl.BlockSpec(memory_space=pltpu.VMEM)
    anywhere = pl.BlockSpec(memory_space=pl.ANY)
    dma = pltpu.SemaphoreType.DMA
    f32, bf16 = jnp.float32, jnp.bfloat16
    pool, where, inverse, factor = pl.pallas_call(
        functools.partial(exchange_kernel, scale),
        name="exchange",
        out_shape=(
            pltpu.VMEM((BAL + PEERS * MOST, BLK, K), bf16),
            jax.ShapeDtypeStruct((8, 128), jnp.int32),
            jax.ShapeDtypeStruct((K, K), bf16),
            jax.ShapeDtypeStruct((K, K), f32),
        ),
        in_specs=[smem, smem, anywhere],
        out_specs=(vmem,) * 4,
        scratch_shapes=[
            pltpu.VMEM((BAL, BLK, K), bf16),
            pltpu.VMEM((CAPB - BAL, BLK, K), bf16),
            pltpu.VMEM((PEERS, MOST, BLK, K), bf16),
            pltpu.VMEM((PEERS, 8, 128), jnp.int32),
            pltpu.VMEM((PEERS, 8, 128), jnp.int32),
            pltpu.VMEM((K, K), f32),
            pltpu.VMEM((GX, SLICE, K), f32),
            pltpu.VMEM((NY, SLICE, K), f32),
            pltpu.VMEM((NZ, SLICE, K), f32),
            pltpu.VMEM((K, K), f32),
            pltpu.VMEM((K, 2 * K), f32),
            pltpu.VMEM((PANEL, 2 * K), f32),
            dma((CHUNKS,)), dma((PEERS,)), dma((PEERS,)), dma((PEERS,)), dma((PEERS,)),
            dma((GX - 1,)), dma((GX - 1,)), dma((NY - 1,)), dma((NY - 1,)), dma((NZ - 1,)), dma((NZ - 1,)),
            dma((GX - 1,)), dma((GX - 1,)),
        ],
        compiler_params=pltpu.CompilerParams(collective_id=0, has_side_effects=True, vmem_limit_bytes=28 << 20),
    )(row_counts, move_list.transpose(2, 0, 1), snapshots.reshape(CAPB, BLK, K))
    basis, r_factor = pl.pallas_call(
        basis_kernel,
        name="project",
        out_shape=(jax.ShapeDtypeStruct((BAL * BLK, K), bf16), jax.ShapeDtypeStruct((K, K), f32)),
        in_specs=[smem, vmem, vmem, vmem],
        out_specs=(anywhere, vmem),
        scratch_shapes=[
            pltpu.VMEM((BAL * BLK, K), bf16),
            dma((FRONT,)),
        ],
        compiler_params=pltpu.CompilerParams(vmem_limit_bytes=16 << 20),
    )(where, pool, inverse, factor)
    return (basis, r_factor)


def solution(mesh):
    in_specs = (P(("gx", "gy"), None), P(("gx", "gy")), P(("gx", "gy"), None, None))
    out_specs = (P(("gx", "gy"), None), P())
    return jax.shard_map(local, mesh=mesh, in_specs=in_specs, out_specs=out_specs, check_vma=False)
```

```python
import functools
import math

import jax
import jax.numpy as jnp
from jax import lax
from jax.experimental import pallas as pl
from jax.experimental.pallas import tpu as pltpu
from jax.sharding import PartitionSpec as P

K = 256
BLK = 128
MOST = 8
BAL = 128
CAPB = 248
CHUNK = MOST * BLK
CHUNKS = CAPB // MOST
FRONT = BAL // MOST
NZ = NY = 4
GX = 8
SLICE = K // GX
PANEL = 32
UNIT = BLK // 2
GROUPS = (2, 1, 1, 1, 3)
MESH = pl.DeviceIdType.MESH
HIGH = lax.Precision.HIGHEST

OFFSETS = [(a, b) for a in (0, 1, 2, -1) for b in (0, 1, 2, -1) if (a, b) != (0, 0)]
PEERS = len(OFFSETS)


def rank_at(rank, dz, dy):
    z, y = lax.div(rank, NY), lax.rem(rank, NY)
    return lax.rem(z + (dz + NZ), NZ) * NY + lax.rem(y + (dy + NY), NY)


def cholesky_panels(work, panel_rows):
    rows = lax.broadcasted_iota(jnp.int32, (PANEL, 1), 0)
    all_rows = lax.broadcasted_iota(jnp.int32, (K, 1), 0)

    def panel_step(panel, carry):
        first = pl.multiple_of(panel * PANEL, PANEL)
        block = work[pl.ds(first, PANEL), :]
        diag = pltpu.roll(block[:, :K], K - first, 1)[:, :128]
        for k in range(PANEL):
            inv = lax.rsqrt(diag[k:k + 1, k:k + 1])
            column = diag[:, k:k + 1] * inv
            diag_row = diag[k:k + 1, :] * inv
            block_row = block[k:k + 1, :] * inv
            factor = jnp.where(rows > k, column, 0.0)
            diag = jnp.where(rows == k, diag_row, diag - factor * diag_row)
            block = jnp.where(rows == k, block_row, block - factor * block_row)
        panel_rows[...] = block
        update = lax.dot_general(panel_rows[:, :K], panel_rows[...], (((0,), (0,)), ((), ())),
                                 precision=HIGH, preferred_element_type=jnp.float32)
        work[...] = work[...] - jnp.where(all_rows >= first + PANEL, update, 0.0)
        work[pl.ds(first, PANEL), :] = block
        return carry

    lax.fori_loop(0, K // PANEL, panel_step, 0)


def exchange_kernel(scale, counts_ref, moves_ref, slab_hbm,
                    pool, where_ref, inverse_ref, factor_ref,
                    front, back, send, count_send, count_recv, gram, gx_recv, y_recv, z_recv, total, work, panel_rows,
                    load_sem, send_sem, recv_sem, cs_sem, cr_sem,
                    gx_s, gx_r, y_s, y_r, z_s, z_r, ag_s, ag_r):
    gx = lax.axis_index("gx")
    gy = lax.axis_index("gy")
    partners = [rank_at(gy, dz, dy) for dz, dy in OFFSETS]
    columns = [lax.rem(gx + d, GX) for d in range(1, GX)]

    def load(chunk, buffer, chunks_before):
        return pltpu.make_async_copy(slab_hbm.at[pl.ds((chunk + chunks_before) * MOST, MOST)],
                                     buffer.at[pl.ds(chunk * MOST, MOST)], load_sem.at[chunk + chunks_before])

    for chunk in range(FRONT):
        load(chunk, front, 0).start()
    barrier = pltpu.get_barrier_semaphore()
    for to in partners:
        pl.semaphore_signal(barrier, inc=1, device_id=(gx, to), device_id_type=MESH)
    for to in columns:
        pl.semaphore_signal(barrier, inc=1, device_id=(to, gy), device_id_type=MESH)

    starts, sent = [], jnp.int32(0)
    for n, to in enumerate(partners):
        start = jnp.int32(0)
        amount = jnp.int32(0)
        for r in range(NZ * NY):
            hit = moves_ref[0, 0, r] == to
            start = start + jnp.where(hit, moves_ref[1, 0, r], 0)
            amount = amount + jnp.where(hit, moves_ref[2, 0, r], 0)
        starts.append(start)
        sent = sent + amount
        count_send[n] = jnp.full((1, 128), amount, jnp.int32)

    pl.semaphore_wait(barrier, PEERS + GX - 1)

    def count_copy(n):
        return pltpu.make_async_remote_copy(
            src_ref=count_send.at[n], dst_ref=count_recv.at[n], send_sem=cs_sem.at[n], recv_sem=cr_sem.at[n],
            device_id=(gx, partners[n]), device_id_type=MESH)

    def block_copy(n, first, blocks):
        return pltpu.make_async_remote_copy(
            src_ref=send.at[n, pl.ds(first, blocks)], dst_ref=pool.at[pl.ds(BAL + n * MOST + first, blocks)],
            send_sem=send_sem.at[n], recv_sem=recv_sem.at[n],
            device_id=(gx, partners[n]), device_id_type=MESH)

    def send_blocks(first, blocks):
        for b in range(first, first + blocks):
            for n in range(PEERS):
                send[n, b] = front[starts[n] + b]
            for part in (pl.ds(0, UNIT), pl.ds(UNIT, UNIT)):
                for n in range(PEERS):
                    pltpu.make_async_remote_copy(
                        src_ref=send.at[n, b, part], dst_ref=pool.at[BAL + n * MOST + b, part],
                        send_sem=send_sem.at[n], recv_sem=recv_sem.at[n],
                        device_id=(gx, partners[n]), device_id_type=MESH).start()

    for chunk in range(FRONT):
        load(chunk, front, 0).wait()
    send_blocks(0, GROUPS[0])
    for chunk in range(CHUNKS - FRONT):
        load(chunk, back, FRONT).start()
    for n in range(PEERS):
        count_copy(n).start()

    valid_rows = counts_ref[0]
    gram[...] = jnp.zeros_like(gram)

    def gram_add(buffer, chunk, chunks_before):
        pieces = []
        for b in range(MOST):
            block = chunk * MOST + b
            keep = jnp.where((block + chunks_before * MOST) * BLK < valid_rows, 1.0, 0.0)
            keep = jnp.full((1, K), keep, jnp.float32).astype(jnp.bfloat16)
            pieces.append(buffer[block] * keep)
        rows = jnp.concatenate(pieces, axis=0)
        gram[...] += lax.dot_general(rows, rows, (((0,), (0,)), ((), ())), preferred_element_type=jnp.float32)

    def gram_front(chunk, carry):
        gram_add(front, chunk, 0)
        return carry

    def gram_back(chunk, carry):
        load(chunk, back, FRONT).wait()
        gram_add(back, chunk, FRONT)
        return carry

    lax.fori_loop(0, FRONT, gram_front, 0)
    lax.fori_loop(0, CHUNKS - FRONT, gram_back, 0)

    def mine(i):
        return pl.ds(pl.multiple_of(i * SLICE, SLICE), SLICE)

    def gx_copy(d):
        to = columns[d - 1]
        return pltpu.make_async_remote_copy(
            src_ref=gram.at[mine(to), :], dst_ref=gx_recv.at[gx], send_sem=gx_s.at[d - 1], recv_sem=gx_r.at[d - 1],
            device_id=(to, gy), device_id_type=MESH)

    for d in range(1, GX):
        gx_copy(d).start()
    send_blocks(GROUPS[0], GROUPS[1])
    gx_recv[gx] = gram[mine(gx), :]
    for d in range(1, GX):
        gx_copy(d).wait()
    part = gx_recv[0]
    for i in range(1, GX):
        part = part + gx_recv[i]

    z, y = lax.div(gy, NY), lax.rem(gy, NY)

    def y_copy(d):
        return pltpu.make_async_remote_copy(
            src_ref=y_recv.at[y], dst_ref=y_recv.at[y], send_sem=y_s.at[d - 1], recv_sem=y_r.at[d - 1],
            device_id=(gx, rank_at(gy, 0, d)), device_id_type=MESH)

    def z_copy(d):
        return pltpu.make_async_remote_copy(
            src_ref=z_recv.at[z], dst_ref=z_recv.at[z], send_sem=z_s.at[d - 1], recv_sem=z_r.at[d - 1],
            device_id=(gx, rank_at(gy, d, 0)), device_id_type=MESH)

    y_recv[y] = part
    for d in range(1, NY):
        y_copy(d).start()
    send_blocks(sum(GROUPS[:2]), GROUPS[2])
    for d in range(1, NY):
        y_copy(d).wait()
    z_recv[z] = (y_recv[0] + y_recv[1]) + (y_recv[2] + y_recv[3])
    for d in range(1, NZ):
        z_copy(d).start()
    send_blocks(sum(GROUPS[:3]), GROUPS[3])
    for d in range(1, NZ):
        z_copy(d).wait()
    total[mine(gx), :] = (z_recv[0] + z_recv[1]) + (z_recv[2] + z_recv[3])

    def ag_copy(d):
        return pltpu.make_async_remote_copy(
            src_ref=total.at[mine(gx), :], dst_ref=total.at[mine(gx), :], send_sem=ag_s.at[d - 1], recv_sem=ag_r.at[d - 1],
            device_id=(columns[d - 1], gy), device_id_type=MESH)

    for d in range(1, GX):
        ag_copy(d).start()
    send_blocks(sum(GROUPS[:4]), GROUPS[4])
    for d in range(1, GX):
        ag_copy(d).wait()

    row = lax.broadcasted_iota(jnp.int32, (K, K), 0)
    col = lax.broadcasted_iota(jnp.int32, (K, K), 1)
    work[:, :K] = total[...]
    work[:, K:] = jnp.where(row == col, 1.0, 0.0)
    cholesky_panels(work, panel_rows)
    factor_ref[...] = jnp.where(col >= row, work[:, :K], 0.0) * (1.0 / scale)
    inverse_ref[...] = (work[:, K:].T * scale).astype(jnp.bfloat16)

    def keep_block(at, carry):
        block = sent + at
        own = jnp.full((1, K), block, jnp.int32) < BAL
        early = front[jnp.minimum(block, BAL - 1)].astype(jnp.float32)
        late = back[jnp.maximum(block - BAL, 0)].astype(jnp.float32)
        pool[at] = jnp.where(own, early, late).astype(jnp.bfloat16)
        return carry

    lax.fori_loop(0, BAL, keep_block, 0)

    for n in range(PEERS):
        count_copy(n).wait()
    position = lax.broadcasted_iota(jnp.int32, (1, 128), 1)
    rest = position - (lax.div(valid_rows, BLK) - sent)
    where = position
    begin = jnp.zeros((1, 128), jnp.int32)
    for j in range(NZ * NY):
        dz = lax.rem(z + (NZ - j // NY), NZ)
        dy = lax.rem(y + (NY - j % NY), NY)
        slot = jnp.int32(0)
        for n, (oz, oy) in enumerate(OFFSETS):
            slot = jnp.where((dz == oz % NZ) & (dy == oy % NY), n, slot)
        amount = jnp.where(gy == j, 0, count_recv[slot])
        inside = rest - begin
        where = jnp.where((inside >= 0) & (inside < amount), BAL + slot * MOST + inside, where)
        begin = begin + amount
    where_ref[...] = where
    for n in range(PEERS):
        block_copy(n, 0, MOST).wait()


def basis_kernel(where_ref, pool, inverse_ref, factor_ref, basis_hbm, r_hbm, out, out_sem, r_sem):
    r_copy = pltpu.make_async_copy(factor_ref, r_hbm, r_sem)
    r_copy.start()

    def out_copy(chunk):
        part = pl.ds(pl.multiple_of(chunk * CHUNK, CHUNK), CHUNK)
        return pltpu.make_async_copy(out.at[part, :], basis_hbm.at[part, :], out_sem.at[chunk])

    def chunk_step(chunk, carry):
        rows = jnp.concatenate([pool[where_ref[0, chunk * MOST + b]] for b in range(MOST)], axis=0)
        out[pl.ds(pl.multiple_of(chunk * CHUNK, CHUNK), CHUNK), :] = jnp.dot(
            rows, inverse_ref[...], preferred_element_type=jnp.float32).astype(jnp.bfloat16)
        out_copy(chunk).start()
        return carry

    lax.fori_loop(0, FRONT, chunk_step, 0, unroll=16)
    for chunk in range(FRONT):
        out_copy(chunk).wait()
    r_copy.wait()


def local(snapshots, row_counts, move_list):
    scale = math.sqrt(lax.axis_size("gx") * lax.axis_size("gy") * BAL * BLK)
    smem = pl.BlockSpec(memory_space=pltpu.SMEM)
    vmem = pl.BlockSpec(memory_space=pltpu.VMEM)
    anywhere = pl.BlockSpec(memory_space=pl.ANY)
    dma = pltpu.SemaphoreType.DMA
    f32, bf16 = jnp.float32, jnp.bfloat16
    pool, where, inverse, factor = pl.pallas_call(
        functools.partial(exchange_kernel, scale),
        name="exchange",
        out_shape=(
            pltpu.VMEM((BAL + PEERS * MOST, BLK, K), bf16),
            jax.ShapeDtypeStruct((1, 128), jnp.int32),
            jax.ShapeDtypeStruct((K, K), bf16),
            jax.ShapeDtypeStruct((K, K), f32),
        ),
        in_specs=[smem, smem, anywhere],
        out_specs=(vmem,) * 4,
        scratch_shapes=[
            pltpu.VMEM((BAL, BLK, K), bf16),
            pltpu.VMEM((CAPB - BAL, BLK, K), bf16),
            pltpu.VMEM((PEERS, MOST, BLK, K), bf16),
            pltpu.VMEM((PEERS, 1, 128), jnp.int32),
            pltpu.VMEM((PEERS, 1, 128), jnp.int32),
            pltpu.VMEM((K, K), f32),
            pltpu.VMEM((GX, SLICE, K), f32),
            pltpu.VMEM((NY, SLICE, K), f32),
            pltpu.VMEM((NZ, SLICE, K), f32),
            pltpu.VMEM((K, K), f32),
            pltpu.VMEM((K, 2 * K), f32),
            pltpu.VMEM((PANEL, 2 * K), f32),
            dma((CHUNKS,)), dma((PEERS,)), dma((PEERS,)), dma((PEERS,)), dma((PEERS,)),
            dma((GX - 1,)), dma((GX - 1,)), dma((NY - 1,)), dma((NY - 1,)), dma((NZ - 1,)), dma((NZ - 1,)),
            dma((GX - 1,)), dma((GX - 1,)),
        ],
        compiler_params=pltpu.CompilerParams(collective_id=0, has_side_effects=True, vmem_limit_bytes=28 << 20),
    )(row_counts, move_list.transpose(2, 0, 1), snapshots.reshape(CAPB, BLK, K))
    basis, r_factor = pl.pallas_call(
        basis_kernel,
        name="project",
        out_shape=(jax.ShapeDtypeStruct((BAL * BLK, K), bf16), jax.ShapeDtypeStruct((K, K), f32)),
        in_specs=[smem, vmem, vmem, vmem],
        out_specs=(anywhere, anywhere),
        scratch_shapes=[
            pltpu.VMEM((BAL * BLK, K), bf16),
            dma((FRONT,)), dma,
        ],
        compiler_params=pltpu.CompilerParams(vmem_limit_bytes=16 << 20),
    )(where, pool, inverse, factor)
    return (basis, r_factor)


def solution(mesh):
    in_specs = (P(("gx", "gy"), None), P(("gx", "gy")), P(("gx", "gy"), None, None))
    out_specs = (P(("gx", "gy"), None), P())
    return jax.shard_map(local, mesh=mesh, in_specs=in_specs, out_specs=out_specs, check_vma=False)
```

```python
import functools
import math

import jax
import jax.numpy as jnp
from jax import lax
from jax.experimental import pallas as pl
from jax.experimental.pallas import tpu as pltpu
from jax.sharding import PartitionSpec as P

K = 256
BLK = 128
MOST = 8
BAL = 128
CAPB = 248
CHUNK = MOST * BLK
CHUNKS = CAPB // MOST
FRONT = BAL // MOST
NZ = NY = 4
GX = 8
SLICE = K // GX
STRIP = SLICE // NY
PANEL = 32
UNIT = BLK // 2
GROUPS = (4, 2, 1, 2, 1, 6)
MESH = pl.DeviceIdType.MESH
HIGH = lax.Precision.HIGHEST

OFFSETS = [(a, b) for a in (0, 1, 2, -1) for b in (0, 1, 2, -1) if (a, b) != (0, 0)]
PEERS = len(OFFSETS)


def rank_at(rank, dz, dy):
    z, y = lax.div(rank, NY), lax.rem(rank, NY)
    return lax.rem(z + (dz + NZ), NZ) * NY + lax.rem(y + (dy + NY), NY)


def cholesky_panels(work, panel_rows):
    rows = lax.broadcasted_iota(jnp.int32, (PANEL, 1), 0)
    all_rows = lax.broadcasted_iota(jnp.int32, (K, 1), 0)

    def panel_step(panel, carry):
        first = pl.multiple_of(panel * PANEL, PANEL)
        block = work[pl.ds(first, PANEL), :]
        diag = pltpu.roll(block[:, :K], K - first, 1)[:, :128]
        for k in range(PANEL):
            inv = lax.rsqrt(diag[k:k + 1, k:k + 1])
            column = diag[:, k:k + 1] * inv
            diag_row = diag[k:k + 1, :] * inv
            block_row = block[k:k + 1, :] * inv
            factor = jnp.where(rows > k, column, 0.0)
            diag = jnp.where(rows == k, diag_row, diag - factor * diag_row)
            block = jnp.where(rows == k, block_row, block - factor * block_row)
        panel_rows[...] = block
        update = lax.dot_general(panel_rows[:, :K], panel_rows[...], (((0,), (0,)), ((), ())),
                                 precision=HIGH, preferred_element_type=jnp.float32)
        work[...] = work[...] - jnp.where(all_rows >= first + PANEL, update, 0.0)
        work[pl.ds(first, PANEL), :] = block
        return carry

    lax.fori_loop(0, K // PANEL, panel_step, 0)


def exchange_kernel(scale, counts_ref, moves_hbm, slab_hbm,
                    pool, where_ref, inverse_ref, factor_ref,
                    moves_ref, front, back, send, count_send, count_recv, gram, gx_recv, part_ref, y_recv, z_recv, total, work, panel_rows,
                    moves_sem, load_sem, send_sem, recv_sem, cs_sem, cr_sem,
                    gx_s, gx_r, y_s, y_r, z_s, z_r, ya_s, ya_r, ag_s, ag_r):
    gx = lax.axis_index("gx")
    gy = lax.axis_index("gy")
    partners = [rank_at(gy, dz, dy) for dz, dy in OFFSETS]
    columns = [lax.rem(gx + d, GX) for d in range(1, GX)]

    def load(chunk, buffer, chunks_before):
        return pltpu.make_async_copy(slab_hbm.at[pl.ds((chunk + chunks_before) * MOST, MOST)],
                                     buffer.at[pl.ds(chunk * MOST, MOST)], load_sem.at[chunk + chunks_before])

    barrier = pltpu.get_barrier_semaphore()
    for to in partners:
        pl.semaphore_signal(barrier, inc=1, device_id=(gx, to), device_id_type=MESH)
    for to in columns:
        pl.semaphore_signal(barrier, inc=1, device_id=(to, gy), device_id_type=MESH)

    moves_copy = pltpu.make_async_copy(moves_hbm, moves_ref, moves_sem)
    moves_copy.start()
    for chunk in range(FRONT):
        load(chunk, front, 0).start()

    moves_copy.wait()

    starts, sent = [], jnp.int32(0)
    for n, to in enumerate(partners):
        start = jnp.int32(0)
        amount = jnp.int32(0)
        for r in range(NZ * NY):
            hit = moves_ref[0, 0, r] == to
            start = start + jnp.where(hit, moves_ref[1, 0, r], 0)
            amount = amount + jnp.where(hit, moves_ref[2, 0, r], 0)
        starts.append(start)
        sent = sent + amount
        count_send[n] = jnp.full((1, 128), amount, jnp.int32)

    pl.semaphore_wait(barrier, PEERS + GX - 1)

    def count_copy(n):
        return pltpu.make_async_remote_copy(
            src_ref=count_send.at[n], dst_ref=count_recv.at[n], send_sem=cs_sem.at[n], recv_sem=cr_sem.at[n],
            device_id=(gx, partners[n]), device_id_type=MESH)

    def block_copy(n, first, blocks):
        return pltpu.make_async_remote_copy(
            src_ref=send.at[n, pl.ds(first, blocks)], dst_ref=pool.at[pl.ds(BAL + n * MOST + first, blocks)],
            send_sem=send_sem.at[n], recv_sem=recv_sem.at[n],
            device_id=(gx, partners[n]), device_id_type=MESH)

    def send_group(group):
        first = sum(GROUPS[:group])
        for unit in range(first, first + GROUPS[group]):
            block, part = unit * UNIT // BLK, pl.ds(unit * UNIT % BLK, UNIT)
            for n in range(PEERS):
                send[n, block, part] = front[starts[n] + block, part]
            for n in range(PEERS):
                pltpu.make_async_remote_copy(
                    src_ref=send.at[n, block, part], dst_ref=pool.at[BAL + n * MOST + block, part],
                    send_sem=send_sem.at[n], recv_sem=recv_sem.at[n],
                    device_id=(gx, partners[n]), device_id_type=MESH).start()

    for chunk in range(FRONT):
        load(chunk, front, 0).wait()
    send_group(0)
    for chunk in range(CHUNKS - FRONT):
        load(chunk, back, FRONT).start()
    for n in range(PEERS):
        count_copy(n).start()

    valid_rows = counts_ref[0]
    gram[...] = jnp.zeros_like(gram)

    def gram_add(buffer, chunk, chunks_before):
        pieces = []
        for b in range(MOST):
            block = chunk * MOST + b
            keep = jnp.where((block + chunks_before * MOST) * BLK < valid_rows, 1.0, 0.0)
            keep = jnp.full((1, K), keep, jnp.float32).astype(jnp.bfloat16)
            pieces.append(buffer[block] * keep)
        rows = jnp.concatenate(pieces, axis=0)
        gram[...] += lax.dot_general(rows, rows, (((0,), (0,)), ((), ())), preferred_element_type=jnp.float32)

    def gram_front(chunk, carry):
        gram_add(front, chunk, 0)
        return carry

    def gram_back(chunk, carry):
        load(chunk, back, FRONT).wait()
        gram_add(back, chunk, FRONT)
        return carry

    lax.fori_loop(0, FRONT, gram_front, 0)
    lax.fori_loop(0, CHUNKS - FRONT, gram_back, 0)

    def mine(i):
        return pl.ds(pl.multiple_of(i * SLICE, SLICE), SLICE)

    def gx_copy(d):
        to = columns[d - 1]
        return pltpu.make_async_remote_copy(
            src_ref=gram.at[mine(to), :], dst_ref=gx_recv.at[gx], send_sem=gx_s.at[d - 1], recv_sem=gx_r.at[d - 1],
            device_id=(to, gy), device_id_type=MESH)

    for d in range(1, GX):
        gx_copy(d).start()
    send_group(1)
    gx_recv[gx] = gram[mine(gx), :]
    for d in range(1, GX):
        gx_copy(d).wait()
    part = gx_recv[0]
    for i in range(1, GX):
        part = part + gx_recv[i]

    z, y = lax.div(gy, NY), lax.rem(gy, NY)

    part_ref[...] = part

    def strip(i):
        return pl.ds(pl.multiple_of(i * STRIP, STRIP), STRIP)

    def y_copy(d):
        to = lax.rem(y + d, NY)
        return pltpu.make_async_remote_copy(
            src_ref=part_ref.at[strip(to), :], dst_ref=y_recv.at[y], send_sem=y_s.at[d - 1], recv_sem=y_r.at[d - 1],
            device_id=(gx, rank_at(gy, 0, d)), device_id_type=MESH)

    my_strip = pl.ds(pl.multiple_of(gx * SLICE + y * STRIP, STRIP), STRIP)

    def ya_copy(d):
        return pltpu.make_async_remote_copy(
            src_ref=total.at[my_strip, :], dst_ref=total.at[my_strip, :], send_sem=ya_s.at[d - 1], recv_sem=ya_r.at[d - 1],
            device_id=(gx, rank_at(gy, 0, d)), device_id_type=MESH)

    def z_copy(d):
        return pltpu.make_async_remote_copy(
            src_ref=z_recv.at[z], dst_ref=z_recv.at[z], send_sem=z_s.at[d - 1], recv_sem=z_r.at[d - 1],
            device_id=(gx, rank_at(gy, d, 0)), device_id_type=MESH)

    y_recv[y] = part_ref[strip(y), :]
    for d in range(1, NY):
        y_copy(d).start()
    send_group(2)
    for d in range(1, NY):
        y_copy(d).wait()
    z_recv[z] = (y_recv[0] + y_recv[1]) + (y_recv[2] + y_recv[3])
    for d in range(1, NZ):
        z_copy(d).start()
    send_group(3)
    for d in range(1, NZ):
        z_copy(d).wait()
    total[my_strip, :] = (z_recv[0] + z_recv[1]) + (z_recv[2] + z_recv[3])
    for d in range(1, NY):
        ya_copy(d).start()
    send_group(4)
    for d in range(1, NY):
        ya_copy(d).wait()

    def ag_copy(d):
        return pltpu.make_async_remote_copy(
            src_ref=total.at[mine(gx), :], dst_ref=total.at[mine(gx), :], send_sem=ag_s.at[d - 1], recv_sem=ag_r.at[d - 1],
            device_id=(columns[d - 1], gy), device_id_type=MESH)

    for d in range(1, GX):
        ag_copy(d).start()
    send_group(5)
    for d in range(1, GX):
        ag_copy(d).wait()

    row = lax.broadcasted_iota(jnp.int32, (K, K), 0)
    col = lax.broadcasted_iota(jnp.int32, (K, K), 1)
    work[:, :K] = total[...]
    work[:, K:] = jnp.where(row == col, 1.0, 0.0)
    cholesky_panels(work, panel_rows)
    factor_ref[...] = jnp.where(col >= row, work[:, :K], 0.0) * (1.0 / scale)
    inverse_ref[...] = (work[:, K:].T * scale).astype(jnp.bfloat16)

    def keep_block(at, carry):
        block = sent + at
        own = jnp.full((1, K), block, jnp.int32) < BAL
        early = front[jnp.minimum(block, BAL - 1)].astype(jnp.float32)
        late = back[jnp.maximum(block - BAL, 0)].astype(jnp.float32)
        pool[at] = jnp.where(own, early, late).astype(jnp.bfloat16)
        return carry

    lax.fori_loop(0, BAL, keep_block, 0)

    for n in range(PEERS):
        count_copy(n).wait()
    position = lax.broadcasted_iota(jnp.int32, (1, 128), 1)
    rest = position - (lax.div(valid_rows, BLK) - sent)
    where = position
    begin = jnp.zeros((1, 128), jnp.int32)
    for j in range(NZ * NY):
        dz = lax.rem(z + (NZ - j // NY), NZ)
        dy = lax.rem(y + (NY - j % NY), NY)
        slot = jnp.int32(0)
        for n, (oz, oy) in enumerate(OFFSETS):
            slot = jnp.where((dz == oz % NZ) & (dy == oy % NY), n, slot)
        amount = jnp.where(gy == j, 0, count_recv[slot])
        inside = rest - begin
        where = jnp.where((inside >= 0) & (inside < amount), BAL + slot * MOST + inside, where)
        begin = begin + amount
    where_ref[...] = where
    for n in range(PEERS):
        block_copy(n, 0, MOST).wait()


def basis_kernel(where_ref, pool, inverse_ref, factor_ref, basis_hbm, r_hbm, out, out_sem, r_sem):
    r_copy = pltpu.make_async_copy(factor_ref, r_hbm, r_sem)
    r_copy.start()

    def out_copy(chunk):
        part = pl.ds(pl.multiple_of(chunk * CHUNK, CHUNK), CHUNK)
        return pltpu.make_async_copy(out.at[part, :], basis_hbm.at[part, :], out_sem.at[chunk])

    def chunk_step(chunk, carry):
        rows = jnp.concatenate([pool[where_ref[0, chunk * MOST + b]] for b in range(MOST)], axis=0)
        out[pl.ds(pl.multiple_of(chunk * CHUNK, CHUNK), CHUNK), :] = jnp.dot(
            rows, inverse_ref[...], preferred_element_type=jnp.float32).astype(jnp.bfloat16)
        out_copy(chunk).start()
        return carry

    lax.fori_loop(0, FRONT, chunk_step, 0, unroll=16)
    for chunk in range(FRONT):
        out_copy(chunk).wait()
    r_copy.wait()


def local(snapshots, row_counts, move_list):
    scale = math.sqrt(lax.axis_size("gx") * lax.axis_size("gy") * BAL * BLK)
    smem = pl.BlockSpec(memory_space=pltpu.SMEM)
    vmem = pl.BlockSpec(memory_space=pltpu.VMEM)
    anywhere = pl.BlockSpec(memory_space=pl.ANY)
    dma = pltpu.SemaphoreType.DMA
    f32, bf16 = jnp.float32, jnp.bfloat16
    pool, where, inverse, factor = pl.pallas_call(
        functools.partial(exchange_kernel, scale),
        name="exchange",
        out_shape=(
            pltpu.VMEM((BAL + PEERS * MOST, BLK, K), bf16),
            jax.ShapeDtypeStruct((1, 128), jnp.int32),
            jax.ShapeDtypeStruct((K, K), bf16),
            jax.ShapeDtypeStruct((K, K), f32),
        ),
        in_specs=[smem, pl.BlockSpec(memory_space=pltpu.HBM), anywhere],
        out_specs=(vmem,) * 4,
        scratch_shapes=[
            pltpu.SMEM((3, 1, NZ * NY), jnp.int32),
            pltpu.VMEM((BAL, BLK, K), bf16),
            pltpu.VMEM((CAPB - BAL, BLK, K), bf16),
            pltpu.VMEM((PEERS, MOST, BLK, K), bf16),
            pltpu.VMEM((PEERS, 1, 128), jnp.int32),
            pltpu.VMEM((PEERS, 1, 128), jnp.int32),
            pltpu.VMEM((K, K), f32),
            pltpu.VMEM((GX, SLICE, K), f32),
            pltpu.VMEM((SLICE, K), f32),
            pltpu.VMEM((NY, STRIP, K), f32),
            pltpu.VMEM((NZ, STRIP, K), f32),
            pltpu.VMEM((K, K), f32),
            pltpu.VMEM((K, 2 * K), f32),
            pltpu.VMEM((PANEL, 2 * K), f32),
            dma, dma((CHUNKS,)), dma((PEERS,)), dma((PEERS,)), dma((PEERS,)), dma((PEERS,)),
            dma((GX - 1,)), dma((GX - 1,)), dma((NY - 1,)), dma((NY - 1,)), dma((NZ - 1,)), dma((NZ - 1,)), dma((NY - 1,)), dma((NY - 1,)),
            dma((GX - 1,)), dma((GX - 1,)),
        ],
        compiler_params=pltpu.CompilerParams(collective_id=0, has_side_effects=True, vmem_limit_bytes=28 << 20),
    )(row_counts, pltpu.with_memory_space_constraint(move_list.transpose(2, 0, 1), pltpu.HBM),
      snapshots.reshape(CAPB, BLK, K))
    basis, r_factor = pl.pallas_call(
        basis_kernel,
        name="project",
        out_shape=(jax.ShapeDtypeStruct((BAL * BLK, K), bf16), jax.ShapeDtypeStruct((K, K), f32)),
        in_specs=[smem, vmem, vmem, vmem],
        out_specs=(anywhere, anywhere),
        scratch_shapes=[
            pltpu.VMEM((BAL * BLK, K), bf16),
            dma((FRONT,)), dma,
        ],
        compiler_params=pltpu.CompilerParams(vmem_limit_bytes=16 << 20),
    )(where, pool, inverse, factor)
    return (basis, r_factor)


def solution(mesh):
    in_specs = (P(("gx", "gy"), None), P(("gx", "gy")), P(("gx", "gy"), None, None))
    out_specs = (P(("gx", "gy"), None), P())
    return jax.shard_map(local, mesh=mesh, in_specs=in_specs, out_specs=out_specs, check_vma=False)
```

```python
import functools
import math

import jax
import jax.numpy as jnp
from jax import lax
from jax.experimental import pallas as pl
from jax.experimental.pallas import tpu as pltpu
from jax.sharding import PartitionSpec as P

K = 256
BLK = 128
MOST = 8
BAL = 128
CAPB = 248
CHUNK = MOST * BLK
CHUNKS = CAPB // MOST
FRONT = BAL // MOST
NZ = NY = 4
GX = 8
SLICE = K // GX
STRIP = SLICE // NY
PANEL = 32
UNIT = BLK // 2
GROUPS = (4, 1, 1, 1, 1, 8)
MESH = pl.DeviceIdType.MESH
HIGH = lax.Precision.HIGHEST

OFFSETS = [(a, b) for a in (0, 1, 2, -1) for b in (0, 1, 2, -1) if (a, b) != (0, 0)]
PEERS = len(OFFSETS)
FAR_FIRST = sorted(range(PEERS), key=lambda n: -abs(OFFSETS[n][0]) - abs(OFFSETS[n][1]))


def rank_at(rank, dz, dy):
    z, y = lax.div(rank, NY), lax.rem(rank, NY)
    return lax.rem(z + (dz + NZ), NZ) * NY + lax.rem(y + (dy + NY), NY)


def cholesky_panels(work, panel_rows):
    rows = lax.broadcasted_iota(jnp.int32, (PANEL, 1), 0)
    all_rows = lax.broadcasted_iota(jnp.int32, (K, 1), 0)

    def panel_step(panel, carry):
        first = pl.multiple_of(panel * PANEL, PANEL)
        block = work[pl.ds(first, PANEL), :]
        diag = pltpu.roll(block[:, :K], K - first, 1)[:, :128]
        for k in range(PANEL):
            inv = lax.rsqrt(diag[k:k + 1, k:k + 1])
            column = diag[:, k:k + 1] * inv
            diag_row = diag[k:k + 1, :] * inv
            block_row = block[k:k + 1, :] * inv
            factor = jnp.where(rows > k, column, 0.0)
            diag = jnp.where(rows == k, diag_row, diag - factor * diag_row)
            block = jnp.where(rows == k, block_row, block - factor * block_row)
        panel_rows[...] = block
        update = lax.dot_general(panel_rows[:, :K], panel_rows[...], (((0,), (0,)), ((), ())),
                                 precision=HIGH, preferred_element_type=jnp.float32)
        work[...] = work[...] - jnp.where(all_rows >= first + PANEL, update, 0.0)
        work[pl.ds(first, PANEL), :] = block
        return carry

    lax.fori_loop(0, K // PANEL, panel_step, 0)


def exchange_kernel(scale, counts_ref, moves_hbm, slab_hbm,
                    pool, where_ref, inverse_ref, factor_ref,
                    moves_ref, front, back, send, count_send, count_recv, gram, gx_recv, part_ref, y_recv, z_recv, total, work, panel_rows,
                    moves_sem, load_sem, send_sem, recv_sem, cs_sem, cr_sem,
                    gx_s, gx_r, y_s, y_r, z_s, z_r, ya_s, ya_r, ag_s, ag_r):
    gx = lax.axis_index("gx")
    gy = lax.axis_index("gy")
    partners = [rank_at(gy, dz, dy) for dz, dy in OFFSETS]
    columns = [lax.rem(gx + d, GX) for d in range(1, GX)]

    def load(chunk, buffer, chunks_before):
        return pltpu.make_async_copy(slab_hbm.at[pl.ds((chunk + chunks_before) * MOST, MOST)],
                                     buffer.at[pl.ds(chunk * MOST, MOST)], load_sem.at[chunk + chunks_before])

    barrier = pltpu.get_barrier_semaphore()
    for to in partners:
        pl.semaphore_signal(barrier, inc=1, device_id=(gx, to), device_id_type=MESH)
    for to in columns:
        pl.semaphore_signal(barrier, inc=1, device_id=(to, gy), device_id_type=MESH)

    moves_copy = pltpu.make_async_copy(moves_hbm, moves_ref, moves_sem)
    moves_copy.start()
    for chunk in range(FRONT):
        load(chunk, front, 0).start()

    moves_copy.wait()

    starts, sent = [], jnp.int32(0)
    for n, to in enumerate(partners):
        start = jnp.int32(0)
        amount = jnp.int32(0)
        for r in range(NZ * NY):
            hit = moves_ref[0, 0, r] == to
            start = start + jnp.where(hit, moves_ref[1, 0, r], 0)
            amount = amount + jnp.where(hit, moves_ref[2, 0, r], 0)
        starts.append(start)
        sent = sent + amount
        count_send[n] = jnp.full((1, 128), amount, jnp.int32)

    pl.semaphore_wait(barrier, PEERS + GX - 1)

    def count_copy(n):
        return pltpu.make_async_remote_copy(
            src_ref=count_send.at[n], dst_ref=count_recv.at[n], send_sem=cs_sem.at[n], recv_sem=cr_sem.at[n],
            device_id=(gx, partners[n]), device_id_type=MESH)

    def block_copy(n, first, blocks):
        return pltpu.make_async_remote_copy(
            src_ref=send.at[n, pl.ds(first, blocks)], dst_ref=pool.at[pl.ds(BAL + n * MOST + first, blocks)],
            send_sem=send_sem.at[n], recv_sem=recv_sem.at[n],
            device_id=(gx, partners[n]), device_id_type=MESH)

    def send_group(group):
        first = sum(GROUPS[:group])
        for unit in range(first, first + GROUPS[group]):
            block, part = unit * UNIT // BLK, pl.ds(unit * UNIT % BLK, UNIT)
            for n in range(PEERS):
                send[n, block, part] = front[starts[n] + block, part]
            for n in FAR_FIRST if unit >= 2 * MOST - 2 else range(PEERS):
                pltpu.make_async_remote_copy(
                    src_ref=send.at[n, block, part], dst_ref=pool.at[BAL + n * MOST + block, part],
                    send_sem=send_sem.at[n], recv_sem=recv_sem.at[n],
                    device_id=(gx, partners[n]), device_id_type=MESH).start()

    for chunk in range(FRONT):
        load(chunk, front, 0).wait()
    send_group(0)
    for chunk in range(CHUNKS - FRONT):
        load(chunk, back, FRONT).start()
    for n in range(PEERS):
        count_copy(n).start()

    valid_rows = counts_ref[0]
    gram[...] = jnp.zeros_like(gram)

    def gram_add(buffer, chunk, chunks_before):
        pieces = []
        for b in range(MOST):
            block = chunk * MOST + b
            keep = jnp.where((block + chunks_before * MOST) * BLK < valid_rows, 1.0, 0.0)
            keep = jnp.full((1, K), keep, jnp.float32).astype(jnp.bfloat16)
            pieces.append(buffer[block] * keep)
        rows = jnp.concatenate(pieces, axis=0)
        gram[...] += lax.dot_general(rows, rows, (((0,), (0,)), ((), ())), preferred_element_type=jnp.float32)

    def gram_front(chunk, carry):
        gram_add(front, chunk, 0)
        return carry

    def gram_back(chunk, carry):
        load(chunk, back, FRONT).wait()
        gram_add(back, chunk, FRONT)
        return carry

    lax.fori_loop(0, FRONT, gram_front, 0)
    lax.fori_loop(0, CHUNKS - FRONT, gram_back, 0)

    def mine(i):
        return pl.ds(pl.multiple_of(i * SLICE, SLICE), SLICE)

    def gx_copy(d):
        to = columns[d - 1]
        return pltpu.make_async_remote_copy(
            src_ref=gram.at[mine(to), :], dst_ref=gx_recv.at[gx], send_sem=gx_s.at[d - 1], recv_sem=gx_r.at[d - 1],
            device_id=(to, gy), device_id_type=MESH)

    for d in range(1, GX):
        gx_copy(d).start()
    send_group(1)
    gx_recv[gx] = gram[mine(gx), :]
    for d in range(1, GX):
        gx_copy(d).wait()
    part = gx_recv[0]
    for i in range(1, GX):
        part = part + gx_recv[i]

    z, y = lax.div(gy, NY), lax.rem(gy, NY)

    part_ref[...] = part

    def strip(i):
        return pl.ds(pl.multiple_of(i * STRIP, STRIP), STRIP)

    def y_copy(d):
        to = lax.rem(y + d, NY)
        return pltpu.make_async_remote_copy(
            src_ref=part_ref.at[strip(to), :], dst_ref=y_recv.at[y], send_sem=y_s.at[d - 1], recv_sem=y_r.at[d - 1],
            device_id=(gx, rank_at(gy, 0, d)), device_id_type=MESH)

    my_strip = pl.ds(pl.multiple_of(gx * SLICE + y * STRIP, STRIP), STRIP)

    def ya_copy(d):
        return pltpu.make_async_remote_copy(
            src_ref=total.at[my_strip, :], dst_ref=total.at[my_strip, :], send_sem=ya_s.at[d - 1], recv_sem=ya_r.at[d - 1],
            device_id=(gx, rank_at(gy, 0, d)), device_id_type=MESH)

    def z_copy(d):
        return pltpu.make_async_remote_copy(
            src_ref=z_recv.at[z], dst_ref=z_recv.at[z], send_sem=z_s.at[d - 1], recv_sem=z_r.at[d - 1],
            device_id=(gx, rank_at(gy, d, 0)), device_id_type=MESH)

    y_recv[y] = part_ref[strip(y), :]
    for d in range(1, NY):
        y_copy(d).start()
    send_group(2)
    for d in range(1, NY):
        y_copy(d).wait()
    z_recv[z] = (y_recv[0] + y_recv[1]) + (y_recv[2] + y_recv[3])
    for d in range(1, NZ):
        z_copy(d).start()
    send_group(3)
    for d in range(1, NZ):
        z_copy(d).wait()
    total[my_strip, :] = (z_recv[0] + z_recv[1]) + (z_recv[2] + z_recv[3])
    for d in range(1, NY):
        ya_copy(d).start()
    send_group(4)
    for d in range(1, NY):
        ya_copy(d).wait()

    def ag_copy(d):
        return pltpu.make_async_remote_copy(
            src_ref=total.at[mine(gx), :], dst_ref=total.at[mine(gx), :], send_sem=ag_s.at[d - 1], recv_sem=ag_r.at[d - 1],
            device_id=(columns[d - 1], gy), device_id_type=MESH)

    for d in range(1, GX):
        ag_copy(d).start()
    send_group(5)
    for d in range(1, GX):
        ag_copy(d).wait()

    row = lax.broadcasted_iota(jnp.int32, (K, K), 0)
    col = lax.broadcasted_iota(jnp.int32, (K, K), 1)
    work[:, :K] = total[...]
    work[:, K:] = jnp.where(row == col, 1.0, 0.0)
    cholesky_panels(work, panel_rows)
    factor_ref[...] = jnp.where(col >= row, work[:, :K], 0.0) * (1.0 / scale)
    inverse_ref[...] = (work[:, K:].T * scale).astype(jnp.bfloat16)

    def keep_block(at, carry):
        block = sent + at
        own = jnp.full((1, K), block, jnp.int32) < BAL
        early = front[jnp.minimum(block, BAL - 1)].astype(jnp.float32)
        late = back[jnp.maximum(block - BAL, 0)].astype(jnp.float32)
        pool[at] = jnp.where(own, early, late).astype(jnp.bfloat16)
        return carry

    lax.fori_loop(0, BAL, keep_block, 0)

    for n in range(PEERS):
        count_copy(n).wait()
    position = lax.broadcasted_iota(jnp.int32, (1, 128), 1)
    rest = position - (lax.div(valid_rows, BLK) - sent)
    where = position
    begin = jnp.zeros((1, 128), jnp.int32)
    for j in range(NZ * NY):
        dz = lax.rem(z + (NZ - j // NY), NZ)
        dy = lax.rem(y + (NY - j % NY), NY)
        slot = jnp.int32(0)
        for n, (oz, oy) in enumerate(OFFSETS):
            slot = jnp.where((dz == oz % NZ) & (dy == oy % NY), n, slot)
        amount = jnp.where(gy == j, 0, count_recv[slot])
        inside = rest - begin
        where = jnp.where((inside >= 0) & (inside < amount), BAL + slot * MOST + inside, where)
        begin = begin + amount
    where_ref[...] = where
    for n in range(PEERS):
        block_copy(n, 0, MOST).wait()


def basis_kernel(where_ref, pool, inverse_ref, factor_ref, basis_hbm, r_hbm, out, out_sem, r_sem):
    r_copy = pltpu.make_async_copy(factor_ref, r_hbm, r_sem)
    r_copy.start()

    def out_copy(chunk):
        part = pl.ds(pl.multiple_of(chunk * CHUNK, CHUNK), CHUNK)
        return pltpu.make_async_copy(out.at[part, :], basis_hbm.at[part, :], out_sem.at[chunk])

    def chunk_step(chunk, carry):
        rows = jnp.concatenate([pool[where_ref[0, chunk * MOST + b]] for b in range(MOST)], axis=0)
        out[pl.ds(pl.multiple_of(chunk * CHUNK, CHUNK), CHUNK), :] = jnp.dot(
            rows, inverse_ref[...], preferred_element_type=jnp.float32).astype(jnp.bfloat16)
        out_copy(chunk).start()
        return carry

    lax.fori_loop(0, FRONT, chunk_step, 0, unroll=16)
    for chunk in range(FRONT):
        out_copy(chunk).wait()
    r_copy.wait()


def local(snapshots, row_counts, move_list):
    scale = math.sqrt(lax.axis_size("gx") * lax.axis_size("gy") * BAL * BLK)
    smem = pl.BlockSpec(memory_space=pltpu.SMEM)
    vmem = pl.BlockSpec(memory_space=pltpu.VMEM)
    anywhere = pl.BlockSpec(memory_space=pl.ANY)
    dma = pltpu.SemaphoreType.DMA
    f32, bf16 = jnp.float32, jnp.bfloat16
    pool, where, inverse, factor = pl.pallas_call(
        functools.partial(exchange_kernel, scale),
        name="exchange",
        out_shape=(
            pltpu.VMEM((BAL + PEERS * MOST, BLK, K), bf16),
            jax.ShapeDtypeStruct((1, 128), jnp.int32),
            jax.ShapeDtypeStruct((K, K), bf16),
            jax.ShapeDtypeStruct((K, K), f32),
        ),
        in_specs=[smem, pl.BlockSpec(memory_space=pltpu.HBM), anywhere],
        out_specs=(vmem,) * 4,
        scratch_shapes=[
            pltpu.SMEM((3, 1, NZ * NY), jnp.int32),
            pltpu.VMEM((BAL, BLK, K), bf16),
            pltpu.VMEM((CAPB - BAL, BLK, K), bf16),
            pltpu.VMEM((PEERS, MOST, BLK, K), bf16),
            pltpu.VMEM((PEERS, 1, 128), jnp.int32),
            pltpu.VMEM((PEERS, 1, 128), jnp.int32),
            pltpu.VMEM((K, K), f32),
            pltpu.VMEM((GX, SLICE, K), f32),
            pltpu.VMEM((SLICE, K), f32),
            pltpu.VMEM((NY, STRIP, K), f32),
            pltpu.VMEM((NZ, STRIP, K), f32),
            pltpu.VMEM((K, K), f32),
            pltpu.VMEM((K, 2 * K), f32),
            pltpu.VMEM((PANEL, 2 * K), f32),
            dma, dma((CHUNKS,)), dma((PEERS,)), dma((PEERS,)), dma((PEERS,)), dma((PEERS,)),
            dma((GX - 1,)), dma((GX - 1,)), dma((NY - 1,)), dma((NY - 1,)), dma((NZ - 1,)), dma((NZ - 1,)), dma((NY - 1,)), dma((NY - 1,)),
            dma((GX - 1,)), dma((GX - 1,)),
        ],
        compiler_params=pltpu.CompilerParams(collective_id=0, has_side_effects=True, vmem_limit_bytes=28 << 20),
    )(row_counts, pltpu.with_memory_space_constraint(move_list.transpose(2, 0, 1), pltpu.HBM),
      snapshots.reshape(CAPB, BLK, K))
    basis, r_factor = pl.pallas_call(
        basis_kernel,
        name="project",
        out_shape=(jax.ShapeDtypeStruct((BAL * BLK, K), bf16), jax.ShapeDtypeStruct((K, K), f32)),
        in_specs=[smem, vmem, vmem, vmem],
        out_specs=(anywhere, anywhere),
        scratch_shapes=[
            pltpu.VMEM((BAL * BLK, K), bf16),
            dma((FRONT,)), dma,
        ],
        compiler_params=pltpu.CompilerParams(vmem_limit_bytes=16 << 20),
    )(where, pool, inverse, factor)
    return (basis, r_factor)


def solution(mesh):
    in_specs = (P(("gx", "gy"), None), P(("gx", "gy")), P(("gx", "gy"), None, None))
    out_specs = (P(("gx", "gy"), None), P())
    return jax.shard_map(local, mesh=mesh, in_specs=in_specs, out_specs=out_specs, check_vma=False)
```
